32 devices in a mesh: rows: 8 (over z, x), canvas: 4 (over y, core).
Axes of the slice: x: 2, y: 2, z: 4, core: 2. Of those that a mesh axis runs over, the one named last changes fastest.
Arguments:
- canvas: bfloat16 [4, 56, 280, 384], P('canvas', 'rows'), may hold values from -6 to 6
- image_ids: int32 [4, 56, 280], P('canvas'), may hold values from 0 to 15679, as said below
- cotangent: bfloat16 [4, 56, 280, 384], P('canvas', 'rows'), may hold values from -6 to 6
- ln1_gain: float32 [384], replicated, may hold values from 0.1 to 1.9
- ln1_bias: float32 [384], replicated, may hold values from -1.75 to 1.75
- qkv_weight: bfloat16 [384, 1152], replicated, may hold values from -0.3125 to 0.3125
- q_bias: float32 [384], replicated, may hold values from -3 to 3
- v_bias: float32 [384], replicated, may hold values from -3 to 3
- bias_table: float32 [169, 12], replicated, may hold values from -6 to 6
- proj_weight: bfloat16 [384, 384], replicated, may hold values from -0.875 to 0.875
- proj_bias: float32 [384], replicated, may hold values from -1.75 to 1.75
- ln2_gain: float32 [384], replicated, may hold values from 0.1 to 1.9
- ln2_bias: float32 [384], replicated, may hold values from -1.75 to 1.75
- fc1_weight: bfloat16 [384, 1536], replicated, may hold values from -0.3125 to 0.3125
- fc1_bias: float32 [1536], replicated, may hold values from -3 to 3
- fc2_weight: bfloat16 [1536, 384], replicated, may hold values from -0.15625 to 0.15625
- fc2_bias: float32 [384], replicated, may hold values from -1.75 to 1.75
Outputs:
- output: bfloat16 [4, 56, 280, 384], P('canvas', 'rows')
- input_grad: bfloat16 [4, 56, 280, 384], P('canvas', 'rows')
- ln1_gain_grad: float32 [384], replicated
- ln1_bias_grad: float32 [384], replicated
- qkv_weight_grad: float32 [384, 1152], replicated
- q_bias_grad: float32 [384], replicated
- v_bias_grad: float32 [384], replicated
- bias_table_grad: float32 [169, 12], replicated
- proj_weight_grad: float32 [384, 384], replicated
- proj_bias_grad: float32 [384], replicated
- ln2_gain_grad: float32 [384], replicated
- ln2_bias_grad: float32 [384], replicated
- fc1_weight_grad: float32 [384, 1536], replicated
- fc1_bias_grad: float32 [1536], replicated
- fc2_weight_grad: float32 [1536, 384], replicated
- fc2_bias_grad: float32 [384], replicated
The draws below stay inside these ranges and needn't reach their ends.
Inputs may be any that keep to these rules, and one draw needn't show every extreme that they name: `image_ids`: every image is a rectangle of tokens with one id; in each canvas one image covers all 56 rows; in each canvas the first token has id 0 and some image has id 56 * 280 - 1.
All inputs are finite; a program needn't handle non-finite values.
Results may differ from the reference program's by a relative error of at most 0.012.
The reference program's roundings to bfloat16 on the way count: a program that leaves them out, or rounds other values in their place, can miss the bound.
Values may be sent and summed in bfloat16 or wider, within the bound.
No kernel may reach another device: no remote copies, remote signals or barrier semaphores. Data moves between devices by JAX's collectives and lax.ppermute only.
A program may use at most 192 MiB of HBM per device.

```python
import math
import jax
import jax.numpy as jnp
from jax import lax

D = 384
HEADS = 12
MLP = 1536
WIN = 7
SHIFT = 3
WINW = 40
TABLE = 169
W = 280
H = 56
CANVASES = 4
N_ROWS = 8


def draw_image_ids(key, part):
    key = jax.random.fold_in(key, 11)
    col_key, row_key, pick_key = jax.random.split(key, 3)
    col_breaks = (jax.random.randint(col_key, (CANVASES, W), 0, 8) == 0).astype(jnp.int32)
    col_breaks = jnp.where(jnp.arange(W)[None, :] == 0, 0, col_breaks)
    strips = jnp.cumsum(col_breaks, axis=1).astype(jnp.int32)
    row_flags = (jax.random.randint(row_key, (CANVASES, H, W), 0, 10) == 0).astype(jnp.int32)
    row_flags = jnp.take_along_axis(row_flags, jnp.broadcast_to(strips[:, None, :], (CANVASES, H, W)), axis=2)
    chosen = jax.random.randint(pick_key, (CANVASES, 1), 0, W)
    tall = jnp.take_along_axis(strips, chosen, axis=1)
    row_flags = jnp.where(strips[:, None, :] == tall[:, :, None], 0, row_flags)
    row_flags = jnp.where(jnp.arange(H)[None, :, None] == 0, 0, row_flags)
    segments = jnp.cumsum(row_flags, axis=1).astype(jnp.int32)
    labels = (strips[:, None, :] * H + segments).astype(jnp.int32)
    largest = jnp.max(labels, axis=(1, 2), keepdims=True)
    return jnp.where(labels == largest, H * W - 1, labels).astype(jnp.int32)


def shard_levels(stream_key, dims, cuts, low, top_value):
    def one(dim, parts):
        heights = jax.random.uniform(jax.random.fold_in(jax.random.fold_in(stream_key, 6), dim), (parts,), jnp.float32, low / len(cuts), top_value / len(cuts))
        return jnp.repeat(jnp.exp(heights), dims[dim] // parts).reshape((-1,) + (1,) * (len(dims) - dim - 1))

    level = one(*cuts[0])
    for cut in cuts[1:]:
        level = level * one(*cut)
    return level


def centred(stream_key, shape, deviation, reach, cuts=(), held_as=jnp.bfloat16):
    level = shard_levels(stream_key, shape, cuts, -0.22, 0.18) if cuts else 1.0
    array = jax.random.normal(stream_key, shape, jnp.float32) * deviation * level
    return jnp.minimum(jnp.maximum(array, -reach), reach).astype(held_as)


def setup_inputs(seed: int = 0) -> dict:
    arg_keys = jax.random.split(jax.random.key(seed), 18)
    canvas = centred(arg_keys[0], (CANVASES, H, W, D), 1.0, 6.0, ((0, 4), (1, 8)))
    image_ids = draw_image_ids(jax.random.fold_in(arg_keys[17], 71), 0)
    cotangent = centred(arg_keys[2], (CANVASES, H, W, D), 1.0, 6.0, ((0, 4), (1, 8)))
    ln1_gain = jnp.clip(1.0 + 0.18 * jax.random.normal(arg_keys[3], (D,), jnp.float32), 0.1, 1.9)
    ln1_bias = centred(arg_keys[4], (D,), 0.3, 1.75, (), jnp.float32)
    qkv_weight = centred(arg_keys[5], (D, 3 * D), D ** -0.5, 0.3125)
    q_bias = centred(arg_keys[6], (D,), 0.5, 3.0, (), jnp.float32)
    v_bias = centred(arg_keys[7], (D,), 0.5, 3.0, (), jnp.float32)
    bias_table = centred(arg_keys[8], (TABLE, HEADS), 1.0, 6.0, (), jnp.float32)
    proj_weight = centred(arg_keys[9], (D, D), (D // 7) ** -0.5, 0.875)
    proj_bias = centred(arg_keys[10], (D,), 0.3, 1.75, (), jnp.float32)
    ln2_gain = jnp.clip(1.0 + 0.18 * jax.random.normal(arg_keys[11], (D,), jnp.float32), 0.1, 1.9)
    ln2_bias = centred(arg_keys[12], (D,), 0.3, 1.75, (), jnp.float32)
    fc1_weight = centred(arg_keys[13], (D, MLP), D ** -0.5, 0.3125)
    fc1_bias = centred(arg_keys[14], (MLP,), 0.5, 3.0, (), jnp.float32)
    fc2_weight = centred(arg_keys[15], (MLP, D), MLP ** -0.5, 0.15625)
    fc2_bias = centred(arg_keys[16], (D,), 0.3, 1.75, (), jnp.float32)
    return {"canvas": canvas, "image_ids": image_ids, "cotangent": cotangent, "ln1_gain": ln1_gain, "ln1_bias": ln1_bias, "qkv_weight": qkv_weight, "q_bias": q_bias, "v_bias": v_bias, "bias_table": bias_table, "proj_weight": proj_weight, "proj_bias": proj_bias, "ln2_gain": ln2_gain, "ln2_bias": ln2_bias, "fc1_weight": fc1_weight, "fc1_bias": fc1_bias, "fc2_weight": fc2_weight, "fc2_bias": fc2_bias}


@jax.custom_vjp
def low(v):
    return lax.optimization_barrier(v.astype(jnp.bfloat16)).astype(jnp.float32)

@jax.custom_vjp
def low_back(v):
    return v

def low_keep(v):
    return (low(v), None)

def low_pass(kept, grad):
    return (grad,)

def back_keep(v):
    return (v, None)

def back_low(kept, grad):
    return (low(grad),)
low.defvjp(low_keep, low_pass)
low_back.defvjp(back_keep, back_low)

def relative_index():
    span = jnp.arange(WIN * WIN)
    row_pos = span // WIN
    col_pos = span % WIN
    return ((row_pos[:, None] - row_pos[None, :] + WIN - 1) * (2 * WIN - 1) + col_pos[:, None] - col_pos[None, :] + WIN - 1).astype(jnp.int32)

def layer_norm(values, gain, offset):
    center = values - lax.optimization_barrier(jnp.mean(values, axis=-1, keepdims=True))
    spread = lax.optimization_barrier(jnp.mean(center * center, axis=-1, keepdims=True))
    return center * lax.rsqrt(spread + 1e-05) * gain + offset

def to_windows(band):
    rest = band.shape[2:]
    return band.reshape((WIN, WINW, WIN) + rest).swapaxes(0, 1).reshape((WINW, WIN * WIN) + rest)

def from_windows(tiles):
    rest = tiles.shape[2:]
    return tiles.reshape((WINW, WIN, WIN) + rest).swapaxes(0, 1).reshape((WIN, WINW * WIN) + rest)

def band_forward(params, band_x, band_ids, band_side):
    ln1_gain, ln1_bias, qkv_weight, q_bias, v_bias, bias_table, proj_weight, proj_bias, ln2_gain, ln2_bias, fc1_weight, fc1_bias, fc2_weight, fc2_bias = params
    highest = lax.Precision.HIGHEST
    head_dim = D // HEADS
    normed = low_back(low(layer_norm(band_x, ln1_gain, ln1_bias)))
    tiles = to_windows(normed)
    query = low_back(low(jnp.dot(tiles, qkv_weight[:, :D], precision=highest) + q_bias))
    keyed = low_back(low(jnp.dot(tiles, qkv_weight[:, D:2 * D], precision=highest)))
    value = low_back(low(jnp.dot(tiles, qkv_weight[:, 2 * D:], precision=highest) + v_bias))
    query = query.reshape(WINW, WIN * WIN, HEADS, head_dim)
    keyed = keyed.reshape(WINW, WIN * WIN, HEADS, head_dim)
    value = value.reshape(WINW, WIN * WIN, HEADS, head_dim)
    table_bias = bias_table[relative_index()].transpose(2, 0, 1)
    tile_ids = to_windows(band_ids)
    tile_side = to_windows(band_side)
    allowed = (tile_ids[:, :, None] == tile_ids[:, None, :]) & (tile_side[:, :, None] == tile_side[:, None, :])
    scores = jnp.einsum('wihd,wjhd->whij', query, keyed, precision=highest) * (1.0 / math.sqrt(head_dim)) + table_bias
    scores = low_back(jnp.where(allowed[:, None], scores, -1000000000.0))
    attn_probs = low(jax.nn.softmax(scores, axis=-1))
    context = jnp.einsum('whij,wjhd->wihd', attn_probs, value, precision=highest).reshape(WINW, WIN * WIN, D)
    context = from_windows(low_back(low(context)))
    branch = low_back(jnp.dot(context, proj_weight, precision=highest) + proj_bias)
    middle = band_x + branch
    normed_two = low_back(low(layer_norm(middle, ln2_gain, ln2_bias)))
    hidden = low_back(jnp.dot(normed_two, fc1_weight, precision=highest) + fc1_bias)
    activated = low(jax.nn.gelu(hidden, approximate=False))
    return middle + jnp.dot(activated, fc2_weight, precision=highest) + fc2_bias

def reference(canvas, image_ids, cotangent, ln1_gain, ln1_bias, qkv_weight, q_bias, v_bias, bias_table, proj_weight, proj_bias, ln2_gain, ln2_bias, fc1_weight, fc1_bias, fc2_weight, fc2_bias):
    params = tuple((item.astype(jnp.float32) for item in (ln1_gain, ln1_bias, qkv_weight, q_bias, v_bias, bias_table, proj_weight, proj_bias, ln2_gain, ln2_bias, fc1_weight, fc1_bias, fc2_weight, fc2_bias)))
    row_side = ((jnp.arange(H) + SHIFT) % H < SHIFT).astype(jnp.int32)
    col_side = ((jnp.arange(W) + SHIFT) % W < SHIFT).astype(jnp.int32)
    side_bands = (row_side[:, None] * 2 + col_side[None, :]).reshape(N_ROWS, WIN, W)

    def one_canvas(totals, inputs):
        picture, ids, upstream = inputs
        rolled = jnp.roll(picture.astype(jnp.float32), (-SHIFT, -SHIFT), (0, 1)).reshape(N_ROWS, WIN, W, D)
        id_bands = jnp.roll(ids, (-SHIFT, -SHIFT), (0, 1)).reshape(N_ROWS, WIN, W)
        up_bands = jnp.roll(upstream.astype(jnp.float32), (-SHIFT, -SHIFT), (0, 1)).reshape(N_ROWS, WIN, W, D)

        def forward(weights, bands):
            step_fn = jax.checkpoint(band_forward)
            return lax.map(lambda pieces: step_fn(weights, pieces[0], pieces[1], pieces[2]), (bands, id_bands, side_bands))
        result, pullback = jax.vjp(forward, params, rolled)
        weight_grads, input_grads = pullback(up_bands)
        totals = jax.tree.map(lambda left, right: left + right, totals, weight_grads)
        result = jnp.roll(result.reshape(H, W, D), (SHIFT, SHIFT), (0, 1)).astype(jnp.bfloat16)
        input_grads = jnp.roll(input_grads.reshape(H, W, D), (SHIFT, SHIFT), (0, 1)).astype(jnp.bfloat16)
        return (totals, (result, input_grads))
    zeros = jax.tree.map(jnp.zeros_like, params)
    totals, outs = lax.scan(one_canvas, zeros, (canvas, image_ids, cotangent))
    g_ln1g, g_ln1b, g_qkv, g_qb, g_vb, g_table, g_proj, g_projb, g_ln2g, g_ln2b, g_fc1, g_fc1b, g_fc2, g_fc2b = totals
    return (outs[0], outs[1], g_ln1g, g_ln1b, g_qkv, g_qb, g_vb, g_table, g_proj, g_projb, g_ln2g, g_ln2b, g_fc1, g_fc1b, g_fc2, g_fc2b)
```

```python
import functools
import math

import jax
import jax.numpy as jnp
from jax import lax
from jax.experimental import pallas as pl
from jax.experimental.pallas import tpu as pltpu
from jax.sharding import PartitionSpec as P
bf=jnp.bfloat16; f32=jnp.float32
WIN=7; SHIFT=3; SLOT=64; LOG2E=1.4426950408889634
NEG=-1e9*LOG2E

def nt(a,b): return lax.dot_general(a,b,(((1,),(1,)),((),())),preferred_element_type=f32)
def nn(a,b): return jnp.dot(a,b,preferred_element_type=f32)
def tn(a,b): return lax.dot_general(a,b,(((0,),(0,)),((),())),preferred_element_type=f32)

def place_matrix(rows, width, nwin, transpose):
    shape=(rows*width, nwin*16) if transpose else (nwin*16, rows*width)
    s=lax.broadcasted_iota(jnp.int32, shape, 1 if transpose else 0)
    t=lax.broadcasted_iota(jnp.int32, shape, 0 if transpose else 1)
    w=s>>4; a=(s>>3)&1; b=s&7
    col=w*WIN+b+SHIFT
    col=jnp.where(col>=width,col-width,col)
    src=jnp.where(b<WIN, a*width+col, -1)
    return jnp.where(src==t, 1.0, 0.0).astype(bf)

def normalized(x):
    c=x-jnp.mean(x,axis=-1,keepdims=True)
    v=jnp.mean(c*c,axis=-1,keepdims=True)
    r=lax.rsqrt(v+1e-5)
    return c*r, r

def k1_body(cw, nsteps, xo_ref, xh_ref, g_ref, b_ref, w_ref, qb_ref, vb_ref, bias_ref, code_ref,
            qkv_ref, p_ref, n1_ref, ctx_ref, n1s, ctxs):
    R,W,D=xo_ref.shape
    NW=W//WIN; keep=R-SHIFT
    scale2=LOG2E/math.sqrt(32.0)
    step=pl.program_id(0)
    @pl.when(step==0)
    def _():
        g=g_ref[...]; b=b_ref[...]
        oh=place_matrix(2,W,NW,False)
        def row(a):
            return (xo_ref[SHIFT+a] if a<keep else xh_ref[a-keep]).astype(f32)
        for k in range(4):
            rows=[row(a) for a in (2*k,2*k+1) if a<R]
            x=jnp.concatenate(rows,axis=0)
            n=normalized(x)[0]*g+b
            s=nn(oh[:,:n.shape[0]],n.astype(bf))
            n1s[:,16*k:16*k+16,:]=s.reshape(NW,16,D).astype(bf)
    base=step*cw
    n=n1s[pl.ds(base,cw)]
    n1_ref[...]=n
    flat=n.reshape(cw*SLOT,D)
    for part in range(3):
        y=nn(flat,w_ref[:,part*D:(part+1)*D])
        if part==0: y=y+qb_ref[...]
        if part==2: y=y+vb_ref[...]
        qkv_ref[:,:,part*D:(part+1)*D]=y.reshape(cw,SLOT,D).astype(bf)
    lane=lax.broadcasted_iota(jnp.int32,(1,128),1)
    hm=[jnp.where((lane>>5)==h,1.0,0.0).astype(bf) for h in range(4)]
    lane64=lax.broadcasted_iota(jnp.int32,(56,128),1)>>5
    codes=code_ref[...]
    codes_t=codes.T
    def win(i,_):
        allowed=codes_t[:56,i:i+1]==codes[i:i+1]
        allowed=jnp.concatenate([allowed,allowed],axis=1)
        for gi in range(D//128):
            q=qkv_ref[i,:,gi*128:(gi+1)*128]
            k=qkv_ref[i,:,D+gi*128:D+(gi+1)*128]
            v=qkv_ref[i,:,2*D+gi*128:2*D+(gi+1)*128]
            qbd=jnp.concatenate([q*hm[h] for h in range(4)],axis=0)
            s=nt(k,qbd)[:56]*scale2+bias_ref[:,gi*256:(gi+1)*256]
            s=jnp.where(allowed,s,NEG)
            m=jnp.max(s,axis=0,keepdims=True)
            e=jnp.exp2(s-m)
            l=jnp.sum(e,axis=0,keepdims=True)
            p=e*(1.0/l)
            p=jnp.concatenate([p,jnp.zeros((8,256),f32)],axis=0).astype(bf)
            p_ref[i,:,gi*256:(gi+1)*256]=p
            o=tn(p,v)
            c=jnp.where(lane64==0,o[0:56],jnp.where(lane64==1,o[64:120],jnp.where(lane64==2,o[128:184],o[192:248])))
            c=jnp.concatenate([c,jnp.zeros((8,128),f32)],axis=0).astype(bf)
            ctxs[base+i,:,gi*128:(gi+1)*128]=c
        return 0
    for i in range(cw): win(i,0)
    @pl.when(step==nsteps-1)
    def _():
        oh=place_matrix(2,W,NW,True)
        for k in range(4):
            rows=2 if 2*k+1<R else 1
            s=ctxs[:,16*k:16*k+16,:].reshape(NW*16,D)
            y=nn(oh[:rows*W],s)
            for r in range(rows):
                ctx_ref[2*k+r]=y[r*W:(r+1)*W].astype(bf)

def k1(xo,xh,g,b,w,qb,vb,bias,codes,cw=8):
    R,W,D=xo.shape; NW=W//WIN; n=NW//cw
    full=lambda a: pl.BlockSpec(a.shape,lambda i:(0,)*a.ndim)
    chunk=lambda c: pl.BlockSpec((cw,)+c,lambda i:(i,0,0))
    return pl.pallas_call(
        functools.partial(k1_body,cw,n),
        grid=(n,),
        in_specs=[full(xo),full(xh),full(g),full(b),full(w),full(qb),full(vb),full(bias),pl.BlockSpec((cw,128),lambda i:(i,0))],
        out_specs=[chunk((SLOT,3*D)),chunk((SLOT,2*D)),chunk((SLOT,D)),pl.BlockSpec((R,W,D),lambda i:(0,0,0))],
        out_shape=[jax.ShapeDtypeStruct((NW,SLOT,3*D),bf),jax.ShapeDtypeStruct((NW,SLOT,2*D),bf),jax.ShapeDtypeStruct((NW,SLOT,D),bf),jax.ShapeDtypeStruct((R,W,D),bf)],
        scratch_shapes=[pltpu.VMEM((NW,SLOT,D),bf),pltpu.VMEM((NW,SLOT,D),bf)],
        compiler_params=pltpu.CompilerParams(vmem_limit_bytes=56*2**20,dimension_semantics=("arbitrary",)),
    )(xo,xh,g,b,w,qb,vb,bias,codes)
VM=pl.BlockSpec(memory_space=pltpu.VMEM)
HC=256
def gelu_parts(h):
    z=jnp.abs(h)*(1/math.sqrt(2.0))
    t=1.0/(1.0+0.3275911*z)
    poly=t*(0.127414796+t*(-0.142248368+t*(0.7107068705+t*(-0.7265760135+t*0.5307027145))))
    E=jnp.exp2(h*h*(-0.5*1.4426950408889634))
    tail=poly*E
    phi=jnp.where(h>=0,1.0-tail,tail)
    return h*phi, phi+h*E*(1/math.sqrt(2*math.pi))

def chunks(R,W):
    return [(k,min(2,R-k),k*W) for k in range(0,R,2)]

def k2_body(xo_ref,xh_ref,do_ref,dh_ref,ctx_ref,pw_ref,pb_ref,g_ref,b_ref,w1_ref,b1_ref,w2_ref,b2_ref,
            out_ref,dmid_ref,dctx_ref,gw1_ref,gw2_ref,gp_ref,small_ref,gb1_ref,
            n2s,n2t,dys,dyt,mids,acts,dhs,dbs,cxs):
    R,W,D=xo_ref.shape; keep=R-SHIFT; T=R*W; TP=n2s.shape[0]; MLP=w1_ref.shape[1]
    def row(o,h,a): return (o[SHIFT+a] if a<keep else h[a-keep])
    g=g_ref[...]; b=b_ref[...]
    for k,n,off in chunks(R,W):
        x=jnp.concatenate([row(xo_ref,xh_ref,a).astype(f32) for a in range(k,k+n)],axis=0)
        c=jnp.concatenate([ctx_ref[a].astype(f32) for a in range(k,k+n)],axis=0).astype(bf)
        dy=jnp.concatenate([row(do_ref,dh_ref,a).astype(f32) for a in range(k,k+n)],axis=0)
        mid=x+nn(c,pw_ref[...])+pb_ref[...]
        mids[off:off+n*W]=mid
        n2=normalized(mid)[0]*g+b
        if off+n*W<TP and k+n==R:
            z=jnp.zeros((TP-T,D),f32)
            n2=jnp.concatenate([n2,z],axis=0); dy=jnp.concatenate([dy,z],axis=0); cc=jnp.concatenate([c.astype(f32),z],axis=0)
            end=TP
        else: cc=c; end=off+n*W
        n2b=n2.astype(bf); dyb=dy.astype(bf)
        n2s[off:end]=n2b; dys[off:end]=dyb; cxs[off:end]=cc.astype(bf)
    n2t[...]=n2s[...].T
    dyt[...]=dys[...].T
    def hid(j,_):
        hc=pl.ds(pl.multiple_of(j*HC,HC),HC)
        w1=w1_ref[:,hc]; w2=w2_ref[hc,:]; b1=b1_ref[:,hc]
        for k in range(0,TP,TP//4):
            rows=slice(k,k+TP//4)
            h=nn(n2s[rows],w1)+b1
            a,gp=gelu_parts(h)
            da=nt(dys[rows],w2)
            acts[rows,hc]=a.astype(bf)
            dhs[rows,hc]=(da*gp).astype(bf)
        gw2_ref[:,hc]=nn(dyt[...],acts[:,hc]).astype(gw2_ref.dtype)
        gw1_ref[:,hc]=nn(n2t[...],dhs[:,hc]).astype(gw1_ref.dtype)
        return 0
    lax.fori_loop(0,MLP//HC,hid,0)
    tot=[jnp.zeros((8,D),f32) for _ in range(4)]
    def fold(v): return jnp.sum(v.reshape(-1,8,D),axis=0)
    for k,n,off in chunks(R,W):
        rows=slice(off,off+n*W)
        if n*W%16: rp=slice(off,TP)
        else: rp=rows
        m=n*W
        mid=mids[rows]
        o=mid+nn(acts[rp],w2_ref[...])[:m]+b2_ref[...]
        for r in range(n): out_ref[k+r]=o[r*W:(r+1)*W].astype(bf)
        dn=nt(dhs[rp],w1_ref[...])[:m].astype(bf).astype(f32)
        xh,r_=normalized(mid)
        dg=dn*g
        dx=r_*(dg-jnp.mean(dg,axis=-1,keepdims=True)-xh*jnp.mean(dg*xh,axis=-1,keepdims=True))
        dy=dys[rp][:m].astype(f32) if m%16==0 else dys[rp].astype(f32)[:m]
        dm=dy+dx
        dbr=dm.astype(bf)
        dbrf=dbr.astype(f32)
        tot[0]+=fold(dn*xh); tot[1]+=fold(dn); tot[2]+=fold(dbrf); tot[3]+=fold(dy)
        for r in range(n): dmid_ref[k+r]=dm[r*W:(r+1)*W]
        if m%16: dbrp=jnp.concatenate([dbrf,jnp.zeros((TP-off-m,D),f32)],axis=0).astype(bf)
        else: dbrp=dbr
        dbs[rp]=dbrp
        dc=nt(dbrp,pw_ref[...])[:m]
        for r in range(n): dctx_ref[k+r]=dc[r*W:(r+1)*W].astype(bf)
    gp_ref[...]=tn(cxs[...],dbs[...]).astype(gp_ref.dtype)
    for i in range(4): small_ref[i:i+1]=jnp.sum(tot[i],axis=0,keepdims=True)
    def bs(j,acc):
        return acc+jnp.sum(dhs[pl.ds(pl.multiple_of(j*16,16),16)].astype(f32).reshape(2,8,MLP),axis=0)
    acc=lax.fori_loop(0,TP//16,bs,jnp.zeros((8,MLP),f32),unroll=4)
    gb1_ref[...]=jnp.sum(acc,axis=0,keepdims=True)

def k2(xo,xh,do,dh,ctx,pw,pb,g,b,w1,b1,w2,b2,gdt=bf):
    R,W,D=xo.shape; T=R*W; TP=-(-T//64)*64; MLP=w1.shape[1]
    sd=jax.ShapeDtypeStruct
    return pl.pallas_call(k2_body,in_specs=[VM]*13,out_specs=[VM]*8,
        out_shape=[sd((R,W,D),bf),sd((R,W,D),f32),sd((R,W,D),bf),sd((D,MLP),gdt),sd((D,MLP),gdt),sd((D,D),gdt),sd((8,D),f32),sd((1,MLP),f32)],
        scratch_shapes=[pltpu.VMEM((TP,D),bf),pltpu.VMEM((D,TP),bf),pltpu.VMEM((TP,D),bf),pltpu.VMEM((D,TP),bf),pltpu.VMEM((T,D),f32),pltpu.VMEM((TP,MLP),bf),pltpu.VMEM((TP,MLP),bf),pltpu.VMEM((TP,D),bf),pltpu.VMEM((TP,D),bf)],
        compiler_params=pltpu.CompilerParams(vmem_limit_bytes=56*2**20))(xo,xh,do,dh,ctx,pw,pb,g,b,w1,b1,w2,b2)
UN=8
def head_blocks(o,lane64):
    return jnp.where(lane64==0,o[0:56],jnp.where(lane64==1,o[64:120],jnp.where(lane64==2,o[128:184],o[192:248])))
def pad64(v): return jnp.concatenate([v,jnp.zeros((8,v.shape[1]),f32)],axis=0).astype(bf)

def table_sums(acc):
    L=acc.shape[1]
    lane=lax.broadcasted_iota(jnp.int32,(8,L),1)
    ai=(lane>>3)&7
    parts=[]
    for da in range(-6,7):
        v=jnp.zeros((8,L),f32)
        for a in range(7):
            if 0<=a-da<7: v=jnp.where(ai==a,acc[8*(a-da):8*(a-da)+8],v)
        parts.append(v)
    V=jnp.concatenate(parts,axis=0)
    r=lax.broadcasted_iota(jnp.int32,(L,128),0); c=lax.broadcasted_iota(jnp.int32,(L,128),1)
    sel=jnp.where((((r>>6)<<3)|(r&7))==c,1.0,0.0).astype(bf)
    def split(x):
        hi=x.astype(bf); return hi,(x-hi.astype(f32)).astype(bf)
    hi,lo=split(V)
    Z=nn(hi,sel)+nn(lo,sel)
    lz=lax.broadcasted_iota(jnp.int32,(104,128),1)&7
    st=jnp.concatenate([jnp.where(lz==bi,Z,0.0) for bi in range(7)],axis=0)
    rr=lax.broadcasted_iota(jnp.int32,(208,728),0); kk=lax.broadcasted_iota(jnp.int32,(208,728),1)
    bi=sum([(kk>=104*m).astype(jnp.int32) for m in range(1,7)])
    loc=kk-104*bi
    perm=jnp.where(((rr>>4)==(loc>>3))&((rr&15)==bi-(loc&7)+6),1.0,0.0).astype(bf)
    hi,lo=split(st)
    out=nn(perm,hi)+nn(perm,lo)
    e=jnp.where((lax.broadcasted_iota(jnp.int32,(16,128),1)>>3)==lax.broadcasted_iota(jnp.int32,(16,128),0),1.0,0.0).astype(bf)
    hi,lo=split(out)
    return nt(e,hi)+nt(e,lo)

def k3_body(qkv_ref,p_ref,n1_ref,dctx_ref,dmid_ref,xo_ref,xh_ref,w_ref,g_ref,b_ref,
            dx_ref,gw_ref,small_ref,tab_ref,dcs,dqs,n1t,acc):
    R,W,D=xo_ref.shape; NW=W//WIN; keep=R-SHIFT; NT_=NW*SLOT
    scale=1.0/math.sqrt(32.0)
    oh=place_matrix(2,W,NW,False)
    for k,n,off in chunks(R,W):
        c=jnp.concatenate([dctx_ref[a].astype(f32) for a in range(k,k+n)],axis=0).astype(bf)
        s=nn(oh[:,:n*W],c)
        dcs[:,8*k:8*k+16,:]=s.reshape(NW,16,D).astype(bf)
    acc[...]=jnp.zeros_like(acc)
    n1t[0:D]=n1_ref[...].reshape(NT_,D).T
    n1t[D:D+16]=jnp.ones((16,NT_),bf)
    lane=lax.broadcasted_iota(jnp.int32,(1,128),1)
    hm=[jnp.where((lane>>5)==h,1.0,0.0).astype(bf) for h in range(4)]
    lane64=lax.broadcasted_iota(jnp.int32,(56,128),1)>>5
    def win(i):
        for gi in range(D//128):
            cs=slice(gi*128,(gi+1)*128); ss=slice(gi*256,(gi+1)*256)
            q=qkv_ref[i,:,gi*128:(gi+1)*128]
            k=qkv_ref[i,:,D+gi*128:D+(gi+1)*128]
            v=qkv_ref[i,:,2*D+gi*128:2*D+(gi+1)*128]
            dc=dcs[i,:,cs]
            p=p_ref[i,:,ss]
            dcbd=jnp.concatenate([dc*hm[h] for h in range(4)],axis=0)
            qbd=jnp.concatenate([q*hm[h] for h in range(4)],axis=0)
            dp=nt(v,dcbd)[:56]
            pf=p.astype(f32)[:56]
            delta=jnp.sum(dp*pf,axis=0,keepdims=True)
            ds=pf*(dp-delta)
            acc[:,ss]+=ds
            dsb=pad64(ds)
            dqs[i,:,2*D+gi*128:2*D+(gi+1)*128]=nn(p,dcbd).astype(bf)
            dqs[i,:,D+gi*128:D+(gi+1)*128]=(nn(dsb,qbd)*scale).astype(bf)
            dq=head_blocks(tn(dsb,k),lane64)*scale
            dqs[i,:,cs]=pad64(dq)
    def wins(t,_):
        for u in range(UN): win(t*UN+u)
        return 0
    lax.fori_loop(0,NW//UN,wins,0)
    flat=dqs[...].reshape(NT_,3*D)
    CB=384
    for c in range(0,3*D,CB):
        y=nn(n1t[...],dqs[:,:,c:c+CB].reshape(NT_,CB))
        gw_ref[:,c:c+CB]=y[:D].astype(gw_ref.dtype)
        small_ref[0:1,c:c+CB]=y[D:D+1]
    RB=NW//5
    for c in range(0,NW,RB):
        y=nt(dqs[c:c+RB].reshape(RB*SLOT,3*D),w_ref[...])
        dcs[c:c+RB]=y.reshape(RB,SLOT,D).astype(bf)
    oht=place_matrix(2,W,NW,True)
    g=g_ref[...]
    tot=[jnp.zeros((8,D),f32) for _ in range(2)]
    def fold(v): return jnp.sum(v.reshape(-1,8,D),axis=0)
    def row(a): return (xo_ref[SHIFT+a] if a<keep else xh_ref[a-keep]).astype(f32)
    for k,n,off in chunks(R,W):
        dn=nn(oht[:n*W],dcs[:,8*k:8*k+16,:].reshape(NW*16,D))
        x=jnp.concatenate([row(a) for a in range(k,k+n)],axis=0)
        xh,r_=normalized(x)
        dg=dn*g
        dx=r_*(dg-jnp.mean(dg,axis=-1,keepdims=True)-xh*jnp.mean(dg*xh,axis=-1,keepdims=True))
        tot[0]+=fold(dn*xh); tot[1]+=fold(dn)
        for r in range(n): dx_ref[k+r]=(dmid_ref[k+r]+dx[r*W:(r+1)*W]).astype(bf)
    for i in range(2): small_ref[1:2,i*D:(i+1)*D]=jnp.sum(tot[i],axis=0,keepdims=True)
    tab_ref[...]=table_sums(acc[...])

def k3(qkv,p,n1,dctx,dmid,xo,xh,w,g,b,gdt=bf):
    R,W,D=xo.shape; NW=W//WIN
    sd=jax.ShapeDtypeStruct
    return pl.pallas_call(k3_body,in_specs=[VM]*10,out_specs=[VM]*4,
        out_shape=[sd((R,W,D),bf),sd((D,3*D),gdt),sd((8,3*D),f32),sd((16,208),f32)],
        scratch_shapes=[pltpu.VMEM((NW,SLOT,D),bf),pltpu.VMEM((NW,SLOT,3*D),bf),pltpu.VMEM((D+16,NW*SLOT),bf),pltpu.VMEM((56,2*D),f32)],
        compiler_params=pltpu.CompilerParams(vmem_limit_bytes=56*2**20))(qkv,p,n1,dctx,dmid,xo,xh,w,g,b)
AXES = ("rows", "canvas")


def exchange(block, mask):
    devices = lax.axis_size("rows") * lax.axis_size("canvas")
    return lax.ppermute(block, AXES, [(i, i ^ mask) for i in range(devices)])


def pick(block, index):
    return lax.dynamic_index_in_dim(block, index, 0, keepdims=False)


def total_of(parts):
    return sum(p.astype(f32) for p in parts).astype(bf)


def summed(block):
    devices = lax.axis_size("rows") * lax.axis_size("canvas")
    here = lax.axis_index("rows") * lax.axis_size("canvas") + lax.axis_index("canvas")
    core = here & 1
    quarter = (here >> 1) & 3
    halves = block.reshape((2, 4) + block.shape[1:])
    got = exchange(pick(halves, 1 - core), 1)
    half = total_of([pick(halves, core), got])
    got = [exchange(pick(half, quarter ^ d), d << 1) for d in (1, 2, 3)]
    piece = total_of([pick(half, quarter)] + got)
    bit = 8
    while bit < devices:
        steps = 4 if bit * 2 < devices else 2
        piece = total_of([piece] + [exchange(piece, d * bit) for d in range(1, steps)])
        bit *= steps
    got = [piece] + [exchange(piece, d << 1) for d in (1, 2, 3)]

    def at(j):
        v = got[3]
        for d in (2, 1, 0):
            v = jnp.where((quarter ^ d) == j, got[d], v)
        return v

    half = jnp.stack([at(j) for j in range(4)])
    other = exchange(half, 1)
    first = jnp.where(core == 0, half, other)
    second = jnp.where(core == 0, other, half)
    return jnp.concatenate([first, second], axis=0)


def band_codes(image_ids, place, band_rows, width):
    ids = image_ids[0]
    height = ids.shape[0]
    ids = jnp.concatenate([ids, ids[:SHIFT]], axis=0)
    ids = lax.dynamic_slice_in_dim(ids, place * band_rows + SHIFT, band_rows, 0)
    row_side = ((place * band_rows + jnp.arange(band_rows) + SHIFT) % height < SHIFT).astype(jnp.int32)
    col_side = (jnp.arange(width) < SHIFT).astype(jnp.int32)
    code = (ids * 4 + row_side[:, None] * 2 + col_side[None, :]).astype(f32)
    code = jnp.roll(code, -SHIFT, 1).reshape(WIN, width // WIN, WIN).swapaxes(0, 1)
    code = jnp.pad(code, ((0, 0), (0, 1), (0, 1)), constant_values=-1.0).reshape(width // WIN, SLOT)
    return jnp.concatenate([code, code], axis=1)


def spread_table(table):
    j = jnp.arange(56)
    i = jnp.arange(SLOT)
    rel = (i[None, :] // 8 - j[:, None] // 8 + WIN - 1) * (2 * WIN - 1) + i[None, :] % 8 - j[:, None] % 8 + WIN - 1
    hot = (rel.reshape(-1)[:, None] == jnp.arange(table.shape[0])[None, :]).astype(f32)
    flat = jnp.dot(hot, table, precision=lax.Precision.HIGHEST)
    return (flat.reshape(56, SLOT, -1).swapaxes(1, 2) * LOG2E).reshape(56, -1)


def on_device(canvas, image_ids, cotangent, ln1_gain, ln1_bias, qkv_weight, q_bias, v_bias, bias_table,
              proj_weight, proj_bias, ln2_gain, ln2_bias, fc1_weight, fc1_bias, fc2_weight, fc2_bias):
    own, dy = canvas[0], cotangent[0]
    R, W, D = own.shape
    keep = R - SHIFT
    n = lax.axis_size("rows")
    place = lax.axis_index("rows")
    up = [((i + 1) % n, i) for i in range(n)]
    down = [(i, (i + 1) % n) for i in range(n)]
    halo = lax.ppermute(own[:SHIFT], "rows", up)
    halo_dy = lax.ppermute(dy[:SHIFT], "rows", up)
    line = lambda v: v.reshape(1, -1)
    codes = band_codes(image_ids, place, R, W)
    bias = spread_table(bias_table)
    qkv, probs, n1, ctx = k1(own, halo, line(ln1_gain), line(ln1_bias), qkv_weight, line(q_bias), line(v_bias), bias, codes)
    out, dmid, dctx, gw1, gw2, gp, small2, gb1 = k2(own, halo, dy, halo_dy, ctx, proj_weight, line(proj_bias), line(ln2_gain), line(ln2_bias),
                                                    fc1_weight, line(fc1_bias), fc2_weight, line(fc2_bias))
    out_back = lax.ppermute(out[keep:], "rows", down)
    output = jnp.concatenate([out_back, out[:keep]], axis=0)[None]
    MLP = gw1.shape[1]

    def column(parts, rows):
        flat = jnp.concatenate([p.reshape(-1) for p in parts]).astype(bf)
        return jnp.pad(flat, (0, rows * 128 - flat.shape[0])).reshape(rows, 128)

    early = jnp.concatenate([gw1, gw2, gp, column([small2[:4], gb1], D)], axis=1)
    early = summed(early.reshape(8, D // 8, -1)).reshape(D, -1)
    dx, gqkv, small1, tab = k3(qkv, probs, n1, dctx, dmid, own, halo, qkv_weight, line(ln1_gain), line(ln1_bias))
    dx_back = lax.ppermute(dx[keep:], "rows", down)
    input_grad = jnp.concatenate([dx_back, dx[:keep]], axis=0)[None]
    late = jnp.concatenate([gqkv, column([small1[:2], tab], D)], axis=1)
    late = summed(late.reshape(8, D // 8, -1)).reshape(D, -1)
    e = early.astype(f32)
    fc1_g, fc2_g, proj_g = e[:, :MLP], e[:, MLP:2 * MLP].T, e[:, 2 * MLP:2 * MLP + D]
    s = e[:, 2 * MLP + D:].reshape(-1)
    ln2_gg, ln2_bg, proj_bg, fc2_bg = (s[i * D:(i + 1) * D] for i in range(4))
    fc1_bg = s[4 * D:4 * D + MLP]
    l = late.astype(f32)
    qkv_g = l[:, :3 * D]
    s = l[:, 3 * D:].reshape(-1)
    q_bg, v_bg, ln1_gg, ln1_bg = s[:D], s[2 * D:3 * D], s[3 * D:4 * D], s[4 * D:5 * D]
    heads = bias_table.shape[1]
    span = 2 * WIN - 1
    t = s[6 * D:6 * D + 16 * 208].reshape(16, span, 16)[:heads, :, :span]
    table_g = t.reshape(heads, span * span).T
    return (output, input_grad, ln1_gg, ln1_bg, qkv_g, q_bg, v_bg, table_g, proj_g, proj_bg, ln2_gg, ln2_bg,
            fc1_g, fc1_bg, fc2_g, fc2_bg)


def solution(mesh):
    tokens = P("canvas", "rows", None, None)
    return jax.shard_map(
        on_device,
        mesh=mesh,
        in_specs=(tokens, P("canvas", None, None), tokens) + (P(),) * 14,
        out_specs=(tokens, tokens) + (P(),) * 14,
        check_vma=False,
    )
```

```python
import functools
import math

import jax
import jax.numpy as jnp
from jax import lax
from jax.experimental import pallas as pl
from jax.experimental.pallas import tpu as pltpu
from jax.sharding import PartitionSpec as P

bf = jnp.bfloat16
f32 = jnp.float32
WIN = 7
SHIFT = 3
SLOT = 64
LOG2E = 1.4426950408889634
NEG = -1e9 * LOG2E
HC = 256
HALVES = 2
UN = 8
BLOCKS = 8
SMALL = 16
AXES = ("rows", "canvas")
VM = pl.BlockSpec(memory_space=pltpu.VMEM)


def nt(a, b):
    return lax.dot_general(a, b, (((1,), (1,)), ((), ())), preferred_element_type=f32)


def nn(a, b):
    return jnp.dot(a, b, preferred_element_type=f32)


def tn(a, b):
    return lax.dot_general(a, b, (((0,), (0,)), ((), ())), preferred_element_type=f32)


def sd(shape, dtype=bf):
    return jax.ShapeDtypeStruct(shape, dtype)


def call(body, outs, scratch, limit, micros, *args, after=()):
    count = len(args)

    def inner(*refs):
        body(*refs[:count], *refs[count + len(after) :])

    return pl.pallas_call(
        inner,
        in_specs=[VM] * count + [pl.BlockSpec(memory_space=pl.ANY)] * len(after),
        out_specs=jax.tree.map(lambda _: VM, outs),
        out_shape=outs,
        scratch_shapes=scratch,
        cost_estimate=pl.CostEstimate(flops=int(micros * 1e9), bytes_accessed=int(micros * 1e6), transcendentals=0),
        compiler_params=pltpu.CompilerParams(vmem_limit_bytes=limit * 2**20),
    )(*args, *after)


def chunks(R, W):
    return [(k, min(2, R - k), k * W) for k in range(0, R, 2)]


def place_matrix(rows, width, nwin, transpose):
    shape = (rows * width, nwin * 16) if transpose else (nwin * 16, rows * width)
    s = lax.broadcasted_iota(jnp.int32, shape, 1 if transpose else 0)
    t = lax.broadcasted_iota(jnp.int32, shape, 0 if transpose else 1)
    w = s >> 4
    a = (s >> 3) & 1
    b = s & 7
    col = w * WIN + b + SHIFT
    col = jnp.where(col >= width, col - width, col)
    src = jnp.where(b < WIN, a * width + col, -1)
    return jnp.where(src == t, 1.0, 0.0).astype(bf)


def normalized(x):
    c = x - jnp.mean(x, axis=-1, keepdims=True)
    r = lax.rsqrt(jnp.mean(c * c, axis=-1, keepdims=True) + 1e-5)
    return c * r, r


def norm_pull(dg, xh, r):
    return r * (dg - jnp.mean(dg, axis=-1, keepdims=True) - xh * jnp.mean(dg * xh, axis=-1, keepdims=True))


def gelu_parts(h):
    z = jnp.abs(h) * (1 / math.sqrt(2.0))
    t = 1.0 / (1.0 + 0.3275911 * z)
    poly = t * (0.127414796 + t * (-0.142248368 + t * (0.7107068705 + t * (-0.7265760135 + t * 0.5307027145))))
    e = jnp.exp2(h * h * (-0.5 * LOG2E))
    tail = poly * e
    phi = jnp.where(h >= 0, 1.0 - tail, tail)
    return h * phi, phi + h * e * (1 / math.sqrt(2 * math.pi))


def head_masks():
    lane = lax.broadcasted_iota(jnp.int32, (1, 128), 1)
    return [jnp.where((lane >> 5) == h, 1.0, 0.0).astype(bf) for h in range(4)]


def head_blocks(o, owner):
    return jnp.where(owner == 0, o[0:56], jnp.where(owner == 1, o[64:120], jnp.where(owner == 2, o[128:184], o[192:248])))


def pad64(v):
    return jnp.concatenate([v, jnp.zeros((8, v.shape[1]), f32)], axis=0).astype(bf)


def band_row(own, halo, a):
    keep = own.shape[0] - SHIFT
    return own[SHIFT + a] if a < keep else halo[a - keep]


def rows_of(own, halo, k, n):
    return jnp.concatenate([band_row(own, halo, a).astype(f32) for a in range(k, k + n)], axis=0)


def position():
    here = lax.axis_index("rows") * lax.axis_size("canvas") + lax.axis_index("canvas")
    return here & 1, (here >> 1) & 3


def ordered(core, d):
    return jnp.where(core == 0, d, ((d & 1) << 1) | (d >> 1))


def deal(block, keep_ref, send_ref):
    core, quarter = position()
    for c in range(4):
        kept, sent = ordered(core, quarter ^ c), ordered(1 - core, quarter ^ c)
        for rows, first, second in block(2 * c, 2 * c + 1):
            keep_ref[kept, rows] = jnp.where(core == 0, first, second).astype(bf)
            send_ref[sent, rows] = jnp.where(core == 0, second, first).astype(bf)


def attend_body(xo_ref, xh_ref, g_ref, b_ref, w_ref, qb_ref, vb_ref, bias_ref, code_ref, qkv_ref, p_ref, hat_ref, ctx_ref, n1s, ctxs):
    R, W, D = xo_ref.shape
    NW = W // WIN
    scale = LOG2E / math.sqrt(32.0)
    g = g_ref[...]
    b = b_ref[...]
    oh = place_matrix(2, W, NW, False)
    for k, n, off in chunks(R, W):
        hat = normalized(rows_of(xo_ref, xh_ref, k, n))[0]
        both = jnp.concatenate([(hat * g + b).astype(bf), hat.astype(bf)], axis=1)
        s = nn(oh[:, : n * W], both)
        n1s[:, 8 * k : 8 * k + 16, :] = s[:, :D].reshape(NW, 16, D).astype(bf)
        hat_ref[:, 8 * k : 8 * k + 16, :] = s[:, D:].reshape(NW, 16, D).astype(bf)
    hm = head_masks()
    owner = lax.broadcasted_iota(jnp.int32, (56, 128), 1) >> 5

    def some(t, _):
        base = t * UN
        flat = n1s[pl.ds(base, UN)].reshape(UN * SLOT, D)
        for part in range(3):
            y = nn(flat, w_ref[:, part * D : (part + 1) * D])
            if part == 0:
                y = y + qb_ref[...]
            if part == 2:
                y = y + vb_ref[...]
            qkv_ref[pl.ds(base, UN), :, part * D : (part + 1) * D] = y.reshape(UN, SLOT, D).astype(bf)
        codes = code_ref[pl.ds(pl.multiple_of(base, UN), UN), :]
        codes_t = codes.T
        for gi in range(D // 128):
            for u in range(UN):
                i = base + u
                q = qkv_ref[i, :, gi * 128 : (gi + 1) * 128]
                k = qkv_ref[i, :, D + gi * 128 : D + (gi + 1) * 128]
                qbd = jnp.concatenate([q * m for m in hm], axis=0)
                s = nt(k, qbd)[:56] * scale + bias_ref[:, gi * 256 : (gi + 1) * 256]
                allowed = codes_t[:56, u : u + 1] == codes[u : u + 1]
                s = jnp.where(jnp.concatenate([allowed, allowed], axis=1), s, NEG)
                e = jnp.exp2(s - jnp.max(s, axis=0, keepdims=True))
                p = e * (1.0 / jnp.sum(e, axis=0, keepdims=True))
                p_ref[i, :, gi * 256 : (gi + 1) * 256] = pad64(p)
        for gi in range(D // 128):
            for u in range(UN):
                i = base + u
                v = qkv_ref[i, :, 2 * D + gi * 128 : 2 * D + (gi + 1) * 128]
                o = tn(p_ref[i, :, gi * 256 : (gi + 1) * 256], v)
                ctxs[i, :, gi * 128 : (gi + 1) * 128] = pad64(head_blocks(o, owner))
        return 0

    lax.fori_loop(0, NW // UN, some, 0)
    oh = place_matrix(2, W, NW, True)
    for k, n, off in chunks(R, W):
        y = nn(oh[: n * W], ctxs[:, 8 * k : 8 * k + 16, :].reshape(NW * 16, D))
        for r in range(n):
            ctx_ref[k + r] = y[r * W : (r + 1) * W].astype(bf)


def attend(own, halo, g, b, w, qb, vb, bias, codes):
    R, W, D = own.shape
    NW = W // WIN
    slots = (NW, SLOT, D)
    return call(
        attend_body,
        [sd((NW, SLOT, 3 * D)), sd((NW, SLOT, 2 * D)), sd(slots), sd((R, W, D))],
        [pltpu.VMEM(slots, bf), pltpu.VMEM(slots, bf)],
        LIMIT[0],
        18,
        own, halo, g, b, w, qb, vb, bias, codes,
    )


def hidden_half(half, n2s, dys, n2t, dyt, w1_ref, b1_ref, w2_ref, acts, dhs, keep_ref, send_ref, gb1_ref, g1s, g2s):
    TP, D = n2s.shape
    wide = acts.shape[1]
    RB = TP // 4
    for j in range(wide // HC):
        lo = half * wide + j * HC
        hc = slice(j * HC, (j + 1) * HC)
        w1 = w1_ref[:, lo : lo + HC]
        w2 = w2_ref[lo : lo + HC, :]
        b1 = b1_ref[:, lo : lo + HC]
        for k in range(0, TP, RB):
            rows = slice(k, k + RB)
            a, slope = gelu_parts(nn(n2s[rows], w1) + b1)
            acts[rows, hc] = a.astype(bf)
            dhs[rows, hc] = (nt(dys[rows], w2) * slope).astype(bf)
        g2s[hc, :] = nn(dyt[...], acts[:, hc]).T.astype(bf)
        y = nn(n2t[...], dhs[:, hc])
        g1s[:, hc] = y[:D].astype(bf)
        gb1_ref[:, hc] = y[D : D + 1]

    n1 = D // BLOCKS
    n2 = wide // BLOCKS

    def block(b0, b1):
        for part in range(wide // D):
            cols = slice(part * D, (part + 1) * D)
            yield slice(part * n1, (part + 1) * n1), g1s[b0 * n1 : (b0 + 1) * n1, cols], g1s[b1 * n1 : (b1 + 1) * n1, cols]
        at = wide // D * n1
        yield slice(at, at + n2), g2s[b0 * n2 : (b0 + 1) * n2, :], g2s[b1 * n2 : (b1 + 1) * n2, :]

    deal(block, keep_ref, send_ref)


def mlp_first_body(xo_ref, xh_ref, do_ref, dh_ref, ctx_ref, pw_ref, pb_ref, g_ref, b_ref, w1_ref, b1_ref, w2_ref,
                   mids, n2s, dys, n2t, dyt, acts, dhs, gb1_ref, keep_ref, send_ref, g1s, g2s):
    R, W, D = xo_ref.shape
    T = R * W
    TP = n2s.shape[0]
    g = g_ref[...]
    b = b_ref[...]
    for k, n, off in chunks(R, W):
        c = jnp.concatenate([ctx_ref[a].astype(f32) for a in range(k, k + n)], axis=0).astype(bf)
        mid = rows_of(xo_ref, xh_ref, k, n) + nn(c, pw_ref[...]) + pb_ref[...]
        mids[off : off + n * W] = mid
        n2 = normalized(mid)[0] * g + b
        dy = rows_of(do_ref, dh_ref, k, n)
        end = off + n * W
        if k + n == R:
            zero = jnp.zeros((TP - T, D), f32)
            n2 = jnp.concatenate([n2, zero], axis=0)
            dy = jnp.concatenate([dy, zero], axis=0)
            end = TP
        n2s[off:end] = n2.astype(bf)
        dys[off:end] = dy.astype(bf)
    n2t[0:D] = n2s[...].T
    n2t[D : D + 16] = jnp.ones((16, TP), bf)
    dyt[...] = dys[...].T
    hidden_half(0, n2s, dys, n2t, dyt, w1_ref, b1_ref, w2_ref, acts, dhs, keep_ref, send_ref, gb1_ref, g1s, g2s)


def mlp_second_body(n2s, dys, n2t, dyt, w1_ref, b1_ref, w2_ref, acts, dhs, gb1_ref, keep_ref, send_ref, g1s, g2s):
    hidden_half(1, n2s, dys, n2t, dyt, w1_ref, b1_ref, w2_ref, acts, dhs, keep_ref, send_ref, gb1_ref, g1s, g2s)


def padded(T):
    return -(-T // 64) * 64


def mlp_first(own, halo, dy, dyh, ctx, pw, pb, g, b, w1, b1, w2):
    R, W, D = own.shape
    T = R * W
    TP = padded(T)
    wide = w1.shape[1] // HALVES
    rows = 2 * wide // BLOCKS
    return call(
        mlp_first_body,
        [sd((T, D), f32), sd((TP, D)), sd((TP, D)), sd((D + 16, TP)), sd((D, TP)), sd((TP, wide)), sd((TP, wide)), sd((1, wide), f32),
         sd((4, rows, D)), sd((4, rows, D))],
        [pltpu.VMEM((D, wide), bf), pltpu.VMEM((wide, D), bf)],
        LIMIT[1],
        17,
        own, halo, dy, dyh, ctx, pw, pb, g, b, w1, b1, w2,
    )


def mlp_second(n2s, dys, n2t, dyt, w1, b1, w2):
    TP, D = n2s.shape
    wide = w1.shape[1] // HALVES
    rows = 2 * wide // BLOCKS
    return call(
        mlp_second_body,
        [sd((TP, wide)), sd((TP, wide)), sd((1, wide), f32), sd((4, rows, D)), sd((4, rows, D))],
        [pltpu.VMEM((D, wide), bf), pltpu.VMEM((wide, D), bf)],
        LIMIT[2],
        11,
        n2s, dys, n2t, dyt, w1, b1, w2,
    )


def fold(v):
    return jnp.sum(v.reshape(-1, 8, v.shape[-1]), axis=0)


def middle_body(mids, dys, d0, d1, ctx_ref, w1_ref, g_ref, pw_ref, dmid_ref, dctx_ref, gp_ref, small_ref, dbs, cxs):
    R, W, D = ctx_ref.shape
    TP = dys.shape[0]
    wide = d0.shape[1]
    g = g_ref[...]
    tot = [jnp.zeros((8, D), f32) for _ in range(4)]
    for k, n, off in chunks(R, W):
        m = n * W
        end = off + m if k + n < R else TP
        dn = (nt(d0[off:end], w1_ref[:, :wide]) + nt(d1[off:end], w1_ref[:, wide:]))[:m].astype(bf).astype(f32)
        xh, r = normalized(mids[off : off + m])
        dy = dys[off:end].astype(f32)[:m]
        dm = dy + norm_pull(dn * g, xh, r)
        dbr = dm.astype(bf).astype(f32)
        for i, v in enumerate((dn * xh, dn, dbr, dy)):
            tot[i] += fold(v)
        c = jnp.concatenate([ctx_ref[a].astype(f32) for a in range(k, k + n)], axis=0)
        if end - off > m:
            zero = jnp.zeros((end - off - m, D), f32)
            dbr = jnp.concatenate([dbr, zero], axis=0)
            c = jnp.concatenate([c, zero], axis=0)
        dbs[off:end] = dbr.astype(bf)
        cxs[off:end] = c.astype(bf)
        dc = nt(dbs[off:end], pw_ref[...])
        for i in range(n):
            dmid_ref[k + i] = dm[i * W : (i + 1) * W]
            dctx_ref[k + i] = dc[i * W : (i + 1) * W].astype(bf)
    gp_ref[...] = nn(cxs[...].T, dbs[...]).astype(bf)
    for i in range(4):
        small_ref[i : i + 1] = jnp.sum(tot[i], axis=0, keepdims=True)


def middle(mids, dys, d0, d1, ctx, w1, g, pw, after):
    R, W, D = ctx.shape
    TP = dys.shape[0]
    return call(
        middle_body,
        [sd((R, W, D), f32), sd((R, W, D)), sd((D, D)), sd((8, D), f32)],
        [pltpu.VMEM((TP, D), bf), pltpu.VMEM((TP, D), bf)],
        LIMIT[3],
        10,
        mids, dys, d0, d1, ctx, w1, g, pw, after=after,
    )


def output_body(mids, a0, a1, w2_ref, b2_ref, out_ref):
    R, W, D = out_ref.shape
    TP = a0.shape[0]
    wide = a0.shape[1]
    for k, n, off in chunks(R, W):
        m = n * W
        end = off + m if k + n < R else TP
        o = mids[off : off + m] + (nn(a0[off:end], w2_ref[:wide, :]) + nn(a1[off:end], w2_ref[wide:, :]))[:m] + b2_ref[...]
        for i in range(n):
            out_ref[k + i] = o[i * W : (i + 1) * W].astype(bf)


def finish_output(mids, a0, a1, w2, b2, like, after):
    return call(output_body, sd(like), [], LIMIT[4], 4, mids, a0, a1, w2, b2, after=after)


def split(x):
    hi = x.astype(bf)
    return hi, (x - hi.astype(f32)).astype(bf)


def table_sums(acc):
    L = acc.shape[1]
    ai = (lax.broadcasted_iota(jnp.int32, (8, L), 1) >> 3) & 7
    parts = []
    for da in range(1 - WIN, WIN):
        v = jnp.zeros((8, L), f32)
        for a in range(WIN):
            if 0 <= a - da < WIN:
                v = jnp.where(ai == a, acc[8 * (a - da) : 8 * (a - da) + 8], v)
        parts.append(v)
    r = lax.broadcasted_iota(jnp.int32, (L, 128), 0)
    c = lax.broadcasted_iota(jnp.int32, (L, 128), 1)
    sel = jnp.where((((r >> 6) << 3) | (r & 7)) == c, 1.0, 0.0).astype(bf)
    hi, lo = split(jnp.concatenate(parts, axis=0))
    z = nn(hi, sel) + nn(lo, sel)
    lz = lax.broadcasted_iota(jnp.int32, (104, 128), 1) & 7
    hi, lo = split(jnp.concatenate([jnp.where(lz == bi, z, 0.0) for bi in range(WIN)], axis=0))
    rr = lax.broadcasted_iota(jnp.int32, (208, 728), 0)
    kk = lax.broadcasted_iota(jnp.int32, (208, 728), 1)
    bi = sum((kk >= 104 * m).astype(jnp.int32) for m in range(1, WIN))
    loc = kk - 104 * bi
    perm = jnp.where(((rr >> 4) == (loc >> 3)) & ((rr & 15) == bi - (loc & 7) + WIN - 1), 1.0, 0.0).astype(bf)
    hi, lo = split(nn(perm, hi) + nn(perm, lo))
    e = jnp.where(
        (lax.broadcasted_iota(jnp.int32, (16, 128), 1) >> 3) == lax.broadcasted_iota(jnp.int32, (16, 128), 0), 1.0, 0.0
    ).astype(bf)
    return nt(e, hi) + nt(e, lo)


def group_pull(gi, qkv_ref, p_ref, dcs, dq_ref, dss, acc):
    NW, _, D3 = qkv_ref.shape
    D = D3 // 3
    scale = 1.0 / math.sqrt(32.0)
    hm = head_masks()
    owner = lax.broadcasted_iota(jnp.int32, (56, 128), 1) >> 5
    acc[...] = jnp.zeros_like(acc)
    cs = slice(gi * 128, (gi + 1) * 128)
    ss = slice(gi * 256, (gi + 1) * 256)

    def spread(x):
        return jnp.concatenate([x * m for m in hm], axis=0)

    def some(t, _):
        for u in range(UG):
            i = t * UG + u
            v = qkv_ref[i, :, 2 * D + gi * 128 : 2 * D + (gi + 1) * 128]
            dp = nt(v, spread(dcs[i, :, cs]))[:56]
            p = p_ref[i, :, ss].astype(f32)[:56]
            ds = p * (dp - jnp.sum(dp * p, axis=0, keepdims=True))
            acc[...] += ds
            dss[u] = pad64(ds)
        for u in range(UG):
            i = t * UG + u
            dq_ref[i, :, 256:384] = nn(p_ref[i, :, ss], spread(dcs[i, :, cs])).astype(bf)
        for u in range(UG):
            i = t * UG + u
            q = qkv_ref[i, :, gi * 128 : (gi + 1) * 128]
            dq_ref[i, :, 128:256] = (nn(dss[u], spread(q)) * scale).astype(bf)
        for u in range(UG):
            i = t * UG + u
            k = qkv_ref[i, :, D + gi * 128 : D + (gi + 1) * 128]
            dq_ref[i, :, 0:128] = pad64(head_blocks(tn(dss[u], k), owner) * scale)
        return 0

    lax.fori_loop(0, NW // UG, some, 0)


UG = 20


def group_weight(gi, w_ref):
    D = w_ref.shape[0]
    return jnp.concatenate([w_ref[:, p * D + gi * 128 : p * D + (gi + 1) * 128] for p in range(3)], axis=1)


def norm_sums(gi, y, w_ref, tot):
    D = w_ref.shape[0]
    w = group_weight(gi, w_ref)
    prod = y[:D] * w.astype(f32)
    tot[0] = tot[0] + (prod[:, 0:128] + prod[:, 128:256] + prod[:, 256:384])
    hi, lo = split(jnp.broadcast_to(y[D : D + 1], (8, 3 * 128)))
    tot[1] = tot[1] + (nt(hi, w) + nt(lo, w))[0:1]


def group_grad(gi, hatt, dq_ref, w_ref, gcol_ref, b_ref, tot):
    NW, _, D = dq_ref.shape
    y = nn(hatt[...], dq_ref[...].reshape(NW * SLOT, D))
    norm_sums(gi, y, w_ref, tot)
    return (y[:D] * gcol_ref[...] + b_ref[...] * y[D : D + 1]).astype(bf), y[D : D + 1]


def pull_first_body(qkv_ref, p_ref, hat_ref, dctx_ref, w_ref, gcol_ref, b_ref, dcs, hatt, dq0, sums_ref, acc0, gain_ref, gs_ref, dss):
    R, W, D = dctx_ref.shape
    NW = W // WIN
    oh = place_matrix(2, W, NW, False)
    for k, n, off in chunks(R, W):
        c = jnp.concatenate([dctx_ref[a].astype(f32) for a in range(k, k + n)], axis=0).astype(bf)
        dcs[:, 8 * k : 8 * k + 16, :] = nn(oh[:, : n * W], c).reshape(NW, 16, D).astype(bf)
    hatt[0:D] = hat_ref[...].reshape(NW * SLOT, D).T
    hatt[D : D + 16] = jnp.ones((16, NW * SLOT), bf)
    group_pull(0, qkv_ref, p_ref, dcs, dq0, dss, acc0)
    tot = [jnp.zeros((D, 128), f32), jnp.zeros((1, D), f32)]
    gs_ref[...], sums_ref[0:1] = group_grad(0, hatt, dq0, w_ref, gcol_ref, b_ref, tot)
    gain_ref[...] = tot[0]
    sums_ref[2:3] = tot[1]


def pull_first(qkv, p, hat, dctx, w, gcol, bcol, after):
    R, W, D = dctx.shape
    NW = W // WIN
    slots = (NW, SLOT, D)
    return call(
        pull_first_body,
        [sd(slots), sd((D + 16, NW * SLOT)), sd(slots), sd((8, D), f32), sd((56, 256), f32), sd((D, 128), f32), sd((D, D))],
        [pltpu.VMEM((UG, SLOT, 256), bf)],
        LIMIT[5],
        7,
        qkv, p, hat, dctx, w, gcol, bcol, after=after,
    )


def pull_next_body(qkv_ref, p_ref, hatt, dcs, gp_ref, w_ref, gcol_ref, b_ref, gain_ref, sums_ref, gs0_ref,
                   dq1, sums1_ref, acc1, gain1_ref, keep_ref, send_ref, dss, gs):
    NW, _, D = dq1.shape
    n1 = D // BLOCKS
    group_pull(1, qkv_ref, p_ref, dcs, dq1, dss, acc1)
    tot = [gain_ref[...], sums_ref[2:3]]
    gs[...], sums1_ref[1:2] = group_grad(1, hatt, dq1, w_ref, gcol_ref, b_ref, tot)
    sums1_ref[0:1] = sums_ref[0:1]
    gain1_ref[...] = tot[0]
    sums1_ref[2:3] = tot[1]

    def block(b0, b1):
        for part, ref in enumerate((gs0_ref, gs, gp_ref)):
            yield slice(part * n1, (part + 1) * n1), ref[b0 * n1 : (b0 + 1) * n1, :], ref[b1 * n1 : (b1 + 1) * n1, :]

    deal(block, keep_ref, send_ref)


def pull_next(qkv, p, hatt, dcs, gp, w, gcol, bcol, gain, sums, gs0, after):
    NW, _, D = dcs.shape
    rows = 3 * D // BLOCKS
    return call(
        pull_next_body,
        [sd(dcs.shape), sd((8, D), f32), sd((56, 256), f32), sd((D, 128), f32), sd((4, rows, D)), sd((4, rows, D))],
        [pltpu.VMEM((UG, SLOT, 256), bf), pltpu.VMEM((D, D), bf)],
        LIMIT[6],
        6,
        qkv, p, hatt, dcs, gp, w, gcol, bcol, gain, sums, gs0, after=after,
    )


def pull_second_body(qkv_ref, p_ref, hatt, dcs, w_ref, gcol_ref, b_ref, acc0, acc1, gain_ref, sums_ref, small_ref, gb0_ref, gb1_ref,
                     dq2, keep_ref, send_ref, dss, gs, acc2, sm):
    NW, _, D = dq2.shape
    n1 = D // BLOCKS
    group_pull(2, qkv_ref, p_ref, dcs, dq2, dss, acc2)
    tot = [gain_ref[...], sums_ref[2:3]]
    gs[...], last = group_grad(2, hatt, dq2, w_ref, gcol_ref, b_ref, tot)
    sm[...] = jnp.zeros_like(sm)
    sm[0:4] = small_ref[0:4]
    wide = gb0_ref.shape[1]
    at = 4
    for ref in (gb0_ref, gb1_ref):
        for c in range(0, wide, D):
            sm[at : at + 1] = ref[:, c : c + D]
            at += 1
    for i in range(2):
        sm[8 + i : 9 + i, 0:128] = sums_ref[0:1, 256 * i : 256 * i + 128]
        sm[8 + i : 9 + i, 128:256] = sums_ref[1:2, 256 * i : 256 * i + 128]
        sm[8 + i : 9 + i, 256:384] = last[:, 256 * i : 256 * i + 128]
    sm[10:11] = jnp.sum(tot[0].T, axis=0, keepdims=True)
    sm[11:12] = tot[1]
    sm[16:32, 0:208] = table_sums(jnp.concatenate([acc0[...], acc1[...], acc2[...]], axis=1))

    def block(b0, b1):
        yield slice(0, n1), gs[b0 * n1 : (b0 + 1) * n1, :], gs[b1 * n1 : (b1 + 1) * n1, :]
        yield slice(n1, n1 + SMALL), sm[b0 * SMALL : (b0 + 1) * SMALL, :], sm[b1 * SMALL : (b1 + 1) * SMALL, :]

    deal(block, keep_ref, send_ref)


def pull_second(qkv, p, hatt, dcs, w, gcol, bcol, acc0, acc1, gain, sums, small, gb0, gb1, after):
    NW, _, D = dcs.shape
    rows = D // BLOCKS + SMALL
    return call(
        pull_second_body,
        [sd(dcs.shape), sd((4, rows, D)), sd((4, rows, D))],
        [pltpu.VMEM((UG, SLOT, 256), bf), pltpu.VMEM((D, D), bf), pltpu.VMEM((56, 256), f32), pltpu.VMEM((BLOCKS * SMALL, D), f32)],
        LIMIT[6],
        6,
        qkv, p, hatt, dcs, w, gcol, bcol, acc0, acc1, gain, sums, small, gb0, gb1, after=after,
    )


def input_body(lo, dq0, dq1, dq2, w_ref, dmid_ref, xo_ref, xh_ref, g_ref, dx_ref, dts):
    R, W, D = xo_ref.shape
    NW = W // WIN
    rows = slice(8 * lo, min(SLOT, 8 * (lo + dx_ref.shape[0] + 1)) // 16 * 16)
    height = rows.stop - rows.start
    ws = [group_weight(gi, w_ref) for gi in range(3)]
    for c in range(0, NW, UN):
        y = sum(nt(dq[c : c + UN, rows, :].reshape(UN * height, D), w) for dq, w in zip((dq0, dq1, dq2), ws))
        dts[c : c + UN] = y.reshape(UN, height, D).astype(bf)
    oht = place_matrix(2, W, NW, True)
    g = g_ref[...]
    for k, n, off in chunks(dx_ref.shape[0], W):
        dn = nn(oht[: n * W], dts[:, 8 * k : 8 * k + 16, :].reshape(NW * 16, D))
        xh, r = normalized(rows_of(xo_ref, xh_ref, lo + k, n))
        dx = norm_pull(dn * g, xh, r)
        for i in range(n):
            dx_ref[k + i] = (dmid_ref[lo + k + i] + dx[i * W : (i + 1) * W]).astype(bf)


def finish_input(lo, count, dq0, dq1, dq2, w, dmid, own, halo, g, after):
    NW = dq0.shape[0]
    return call(
        functools.partial(input_body, lo),
        sd((count,) + own.shape[1:]),
        [pltpu.VMEM((NW, SLOT // 2, own.shape[2]), bf)],
        LIMIT[7],
        4,
        dq0, dq1, dq2, w, dmid, own, halo, g, after=after,
    )


def exchange(block, mask):
    devices = lax.axis_size("rows") * lax.axis_size("canvas")
    return lax.ppermute(block, AXES, [(i, i ^ mask) for i in range(devices)])


def alternate(block, first):
    devices = lax.axis_size("rows") * lax.axis_size("canvas")
    return lax.ppermute(block, AXES, [(i, i ^ (4 if (i & 1 == 0) == first else 2)) for i in range(devices)])


def add_half_body(keep_ref, got_ref, kept, sent):
    v = keep_ref[...].astype(f32) + got_ref[...].astype(f32)
    kept[...] = v[0:2].astype(bf)
    sent[...] = v[2:4].astype(bf)


def add_pair_body(kept_ref, got_ref, kept, sent):
    v = kept_ref[...].astype(f32) + got_ref[...].astype(f32)
    kept[...] = v[0].astype(bf)
    sent[...] = v[1].astype(bf)


def add_body(one, two, out):
    out[...] = (one[...].astype(f32) + two[...].astype(f32)).astype(bf)


def join_body(one, two, out):
    n = out.shape[0] // 2
    out[0:n] = one[...].reshape((n,) + out.shape[1:])
    out[n:] = two[...].reshape((n,) + out.shape[1:])


def add_half(keep, got, after=()):
    shape = (2,) + keep.shape[1:]
    return call(add_half_body, [sd(shape)] * 2, [], 2, 1, keep, got, after=after)


def add_pair(kept, got, after=()):
    return call(add_pair_body, [sd(kept.shape[1:])] * 2, [], 2, 1, kept, got, after=after)


def add_piece(one, two, after=()):
    return call(add_body, sd(one.shape), [], 2, 1, one, two, after=after)


def join(one, two, after=()):
    shape = (2,) + one.shape if one.ndim == 2 else (2 * one.shape[0],) + one.shape[1:]
    return call(join_body, sd(shape), [], 2, 1, one, two, after=after)


class Sum:
    def __init__(self, keep, send):
        devices = lax.axis_size("rows") * lax.axis_size("canvas")
        self.bits = [b for b in (2**i for i in range(3, 30)) if b < devices]
        self.at = 0
        self.have, self.got = keep, exchange(send, 1)

    def step(self, after=()):
        n = len(self.bits)
        if self.at == 0:
            self.have, sent = add_half(self.have, self.got, after)
            self.got = alternate(sent, True)
        elif self.at == 1:
            self.have, sent = add_pair(self.have, self.got, after)
            self.got = alternate(sent, False)
        elif self.at < 3 + n:
            self.have = add_piece(self.have, self.got, after)
            self.got = exchange(self.have, self.bits[self.at - 2]) if self.at < 2 + n else alternate(self.have, False)
        elif self.at == 3 + n:
            self.have = join(self.have, self.got, after)
            self.got = alternate(self.have, True)
        elif self.at == 4 + n:
            self.have = join(self.have, self.got, after)
            self.got = exchange(self.have, 1)
        else:
            return None
        self.at += 1
        return self.have

    def finish(self):
        while self.at < 5 + len(self.bits):
            self.step()
        return [self.have, self.got]


def placed():
    core, quarter = position()
    for side in range(2):
        owner = core if side == 0 else 1 - core
        for e in range(4):
            yield side, e, ((quarter ^ ordered(owner, jnp.int32(e))) << 1) | owner


def gather_mlp_body(a0, a1, b0, b1, g1_ref, g2_ref):
    D, MLP = g1_ref.shape
    wide = MLP // HALVES
    n1, n2 = D // BLOCKS, wide // BLOCKS
    for side, e, b in placed():
        for half, pair in enumerate(((a0, a1), (b0, b1))):
            v = pair[side].at[e]
            for part in range(wide // D):
                cols = slice(half * wide + part * D, half * wide + (part + 1) * D)
                g1_ref[pl.ds(pl.multiple_of(b * n1, 8), n1), cols] = v[part * n1 : (part + 1) * n1, :].astype(f32)
            at = wide // D * n1
            g2_ref[pl.ds(pl.multiple_of(half * wide + b * n2, 8), n2), :] = v[at : at + n2, :].astype(f32)


def gather_mlp(a, b, D, MLP):
    return call(gather_mlp_body, [sd((D, MLP), f32), sd((MLP, D), f32)], [], 10, 3, *a, *b)


def gather_late_body(c0, c1, d0, d1, gq_ref, gp_ref, sm_ref, tab_ref):
    D = gp_ref.shape[0]
    n1 = D // BLOCKS
    for side, e, b in placed():
        first, second = (c0, c1)[side].at[e], (d0, d1)[side].at[e]
        rows = pl.ds(pl.multiple_of(b * n1, 8), n1)
        for gi in range(3):
            v = first[gi * n1 : (gi + 1) * n1, :] if gi < 2 else second[0:n1, :]
            for p in range(3):
                gq_ref[rows, p * D + gi * 128 : p * D + (gi + 1) * 128] = v[:, p * 128 : (p + 1) * 128].astype(f32)
        gp_ref[rows, :] = first[2 * n1 : 3 * n1, :].astype(f32)
        sm_ref[pl.ds(pl.multiple_of(b * SMALL, 8), SMALL), :] = second[n1 : n1 + SMALL, :].astype(f32)
    t = sm_ref[16:32, 0:256].T
    heads = tab_ref.shape[1]
    span = 2 * WIN - 1
    for da in range(span):
        tab_ref[da * span : (da + 1) * span, :] = t[da * 16 : da * 16 + span, :heads]


def gather_late(a, b, D, table):
    return call(gather_late_body, [sd((D, 3 * D), f32), sd((D, D), f32), sd((BLOCKS * SMALL, D), f32), sd(table, f32)], [], 10, 3, *a, *b)


def band_codes(image_ids, place, band_rows, width):
    ids = image_ids[0]
    height = ids.shape[0]
    ids = jnp.concatenate([ids, ids[:SHIFT]], axis=0)
    ids = lax.dynamic_slice_in_dim(ids, place * band_rows + SHIFT, band_rows, 0)
    row_side = ((place * band_rows + jnp.arange(band_rows) + SHIFT) % height < SHIFT).astype(jnp.int32)
    col_side = (jnp.arange(width) < SHIFT).astype(jnp.int32)
    code = (ids * 4 + row_side[:, None] * 2 + col_side[None, :]).astype(f32)
    code = jnp.roll(code, -SHIFT, 1).reshape(WIN, width // WIN, WIN).swapaxes(0, 1)
    code = jnp.pad(code, ((0, 0), (0, 1), (0, 1)), constant_values=-1.0).reshape(width // WIN, SLOT)
    return jnp.concatenate([code, code], axis=1)


def spread_table(table):
    j = jnp.arange(56)
    i = jnp.arange(SLOT)
    rel = (i[None, :] // 8 - j[:, None] // 8 + WIN - 1) * (2 * WIN - 1) + i[None, :] % 8 - j[:, None] % 8 + WIN - 1
    hot = (rel.reshape(-1)[:, None] == jnp.arange(table.shape[0])[None, :]).astype(f32)
    flat = jnp.dot(hot, table, precision=lax.Precision.HIGHEST)
    return (flat.reshape(56, SLOT, -1).swapaxes(1, 2) * LOG2E).reshape(56, -1)


LIMIT = [12, 6, 6, 6, 6, 6, 6, 8]


def on_device(canvas, image_ids, cotangent, ln1_gain, ln1_bias, qkv_weight, q_bias, v_bias, bias_table,
              proj_weight, proj_bias, ln2_gain, ln2_bias, fc1_weight, fc1_bias, fc2_weight, fc2_bias):
    own, dy = canvas[0], cotangent[0]
    R, W, D = own.shape
    MLP = fc1_weight.shape[1]
    keep = R - SHIFT
    n = lax.axis_size("rows")
    place = lax.axis_index("rows")
    up = [((i + 1) % n, i) for i in range(n)]
    down = [(i, (i + 1) % n) for i in range(n)]

    def line(v):
        return v.reshape(1, -1)

    def column(v):
        return jnp.broadcast_to(v[:, None], (D, D))

    halo = lax.ppermute(own[:SHIFT], "rows", up)
    halo_dy = lax.ppermute(dy[:SHIFT], "rows", up)
    codes = band_codes(image_ids, place, R, W)
    bias = spread_table(bias_table)
    qkv, probs, hat, ctx = attend(own, halo, line(ln1_gain), line(ln1_bias), qkv_weight, line(q_bias), line(v_bias), bias, codes)
    mids, n2s, dys, n2t, dyt, a0, d0, gb0, keep_a, send_a = mlp_first(
        own, halo, dy, halo_dy, ctx, proj_weight, line(proj_bias), line(ln2_gain), line(ln2_bias), fc1_weight, line(fc1_bias), fc2_weight)
    sum_a = Sum(keep_a, send_a)
    a1, d1, gb1, keep_b, send_b = mlp_second(n2s, dys, n2t, dyt, fc1_weight, line(fc1_bias), fc2_weight)
    sum_b = Sum(keep_b, send_b)
    steps = [sum_a.step()]
    out = finish_output(mids, a0, a1, fc2_weight, line(fc2_bias), own.shape, steps)
    out_back = lax.ppermute(out[keep:], "rows", down)
    steps = [sum_a.step([out]), sum_b.step([out])]
    dmid, dctx, gp, small = middle(mids, dys, d0, d1, ctx, fc1_weight, line(ln2_gain), proj_weight, steps)
    steps = [sum_a.step([dctx]), sum_b.step([dctx])]
    gcol, bcol = column(ln1_gain), column(ln1_bias)
    dcs, hatt, dq0, sums, acc0, gain, gs0 = pull_first(qkv, probs, hat, dctx, qkv_weight, gcol, bcol, steps)
    steps = [sum_a.step([gs0]), sum_b.step([gs0])]
    dq1, sums, acc1, gain, keep_c, send_c = pull_next(qkv, probs, hatt, dcs, gp, qkv_weight, gcol, bcol, gain, sums, gs0, steps + [out_back])
    sum_c = Sum(keep_c, send_c)
    steps = [sum_a.step([keep_c]), sum_b.step([keep_c])]
    dq2, keep_d, send_d = pull_second(
        qkv, probs, hatt, dcs, qkv_weight, gcol, bcol, acc0, acc1, gain, sums, small, gb0, gb1, steps)
    sum_d = Sum(keep_d, send_d)
    steps = [sum_a.step([keep_d]), sum_b.step([keep_d]), sum_c.step([keep_d])]
    dx_next = finish_input(keep, SHIFT, dq0, dq1, dq2, qkv_weight, dmid, own, halo, line(ln1_gain), steps)
    dx_back = lax.ppermute(dx_next, "rows", down)
    steps = [sum_d.step([dx_next])]
    dx_own = finish_input(0, keep, dq0, dq1, dq2, qkv_weight, dmid, own, halo, line(ln1_gain), steps)
    sum_d.step([dx_own])
    parts = [v.finish() for v in (sum_a, sum_b, sum_c, sum_d)]
    input_grad = jnp.concatenate([dx_back, dx_own], axis=0)[None]
    output = jnp.concatenate([out_back, out[:keep]], axis=0)[None]
    fc1_g, fc2_g = gather_mlp(parts[0], parts[1], D, MLP)
    qkv_g, proj_g, sm, table_g = gather_late(parts[2], parts[3], D, bias_table.shape)
    return (output, input_grad, sm[10], sm[11], qkv_g, sm[8], sm[9], table_g, proj_g, sm[2], sm[0], sm[1],
            fc1_g, sm[4:8].reshape(-1), fc2_g, sm[3])


def solution(mesh):
    tokens = P("canvas", "rows", None, None)
    return jax.shard_map(
        on_device,
        mesh=mesh,
        in_specs=(tokens, P("canvas", None, None), tokens) + (P(),) * 14,
        out_specs=(tokens, tokens) + (P(),) * 14,
        check_vma=False,
    )
```
